512 devices in a mesh: dp: 32 (over z, y_hi, core), fsdp: 16 (over y_lo, x).
Axes of the slice: x: 4, y: 8 (y_hi: 2, y_lo: 4; y = y_hi * 4 + y_lo), z: 8, core: 2. Of those that a mesh axis runs over, the one named last changes fastest.
Arguments:
- logits: bfloat16 [16384, 32000], P('dp', 'fsdp'), may hold values from -115 to 125
- labels: int32 [16384], P('dp'), may hold values from 0 to 31999
- activations: bfloat16 [16384, 5120], P('dp', 'fsdp'), may hold values from -6 to 6
- proj_in: bfloat16 [5120, 64], P('fsdp'), may hold values from -0.078125 to 0.078125
- proj_out: bfloat16 [32000, 64], P('fsdp'), may hold values from -6 to 6
Outputs:
- features: float32 [2048, 4096], P(('dp', 'fsdp'))
- gram: float32 [4096, 4096], P('fsdp', 'dp')
The draws below stay inside these ranges and needn't reach their ends.
All inputs are finite; a program needn't handle non-finite values.
Results may differ from the reference program's by a relative error of at most 0.014.
Values may be sent and summed in bfloat16 or wider, within the bound.
A program may use at most 64 MiB of HBM per device.

```python
import jax
import jax.numpy as jnp
from jax import lax

D = 5120
V = 32000
K_IN = 64
K_OUT = 64
SEQ = 8
EX_DEV = 64
FEAT = 4096
EXAMPLES = 2048
TOKENS = 16384
N_DP = 32


def draw_logits(key, part):
    first = jax.random.fold_in(jax.random.fold_in(key, 11), 0)
    base = jnp.clip(3.0 * jax.random.normal(first, (TOKENS, V), jnp.float32), -15.0, 15.0)
    return base.astype(jnp.bfloat16)


def set_ends(values, rng, least, top_value):
    longest = values.shape.index(max(values.shape))
    spots = []
    for shift in (0, 1):
        where = [jax.random.randint(jax.random.fold_in(rng, axis), (), 0, length) for axis, length in enumerate(values.shape)]
        where[longest] = (where[longest] + shift) % values.shape[longest]
        spots.append(tuple(where))
    return values.at[spots[0]].set(least).at[spots[1]].set(top_value)


def steps_of(own_key, dims, cuts, smallest, top_value):
    gain = 1.0
    for position, shards_of in cuts:
        steps = jax.random.uniform(jax.random.fold_in(jax.random.fold_in(own_key, 6), position), (shards_of,), jnp.float32, smallest / len(cuts), top_value / len(cuts))
        gain = gain * jnp.repeat(jnp.exp(steps), dims[position] // shards_of).reshape((-1,) + (1,) * (len(dims) - 1 - position))
    return gain


def gaussian(key, dims, scale, reach, shards=(), kind=jnp.bfloat16):
    drawn = scale * jax.random.normal(key, dims, jnp.float32)
    if shards:
        drawn = drawn * steps_of(key, dims, shards, -0.22, 0.18)
    return jnp.clip(drawn, -reach, reach).astype(kind)


def setup_inputs(seed: int = 0) -> dict:
    seeds = jax.random.split(jax.random.key(seed), 6)
    logits = draw_logits(jax.random.fold_in(seeds[5], 71), 0)
    labels = set_ends(jax.random.randint(seeds[1], (TOKENS,), 0, V), jax.random.fold_in(seeds[1], 1), 0, V - 1).astype(jnp.int32)
    activations = gaussian(seeds[2], (TOKENS, D), 1.0, 6.0, ((0, 32), (1, 16)))
    proj_in = gaussian(seeds[3], (D, K_IN), D ** -0.5, 0.078125, ((0, 16),))
    proj_out = gaussian(seeds[4], (V, K_OUT), 1.0, 6.0, ((0, 16),))
    return {"logits": logits, "labels": labels, "activations": activations, "proj_in": proj_in, "proj_out": proj_out}


def reference(logits, labels, activations, proj_in, proj_out):
    tok_dev = EX_DEV * SEQ
    blocks_logits = logits.reshape(N_DP, tok_dev, V)
    blocks_labels = labels.reshape(N_DP, tok_dev)
    blocks_act = activations.reshape(N_DP, tok_dev, D)

    def one_block(items):
        block_logits, block_labels, block_act = items
        values = block_logits.astype(jnp.float32)
        top = jnp.max(values, axis=1, keepdims=True)
        expo = jnp.exp(values - top)
        prob = expo / jnp.sum(expo, axis=1, keepdims=True)
        columns = lax.broadcasted_iota(jnp.int32, (1, V), 1)
        onehot = (columns == block_labels[:, None]).astype(jnp.float32)
        errors = (prob - onehot).astype(jnp.bfloat16)
        left = jnp.dot(block_act, proj_in, preferred_element_type=jnp.float32)
        right = jnp.dot(errors, proj_out, preferred_element_type=jnp.float32)
        sketch = jnp.einsum("esi,esj->eij", left.reshape(EX_DEV, SEQ, K_IN), right.reshape(EX_DEV, SEQ, K_OUT))
        return sketch.reshape(EX_DEV, K_IN * K_OUT)

    features = lax.map(one_block, (blocks_logits, blocks_labels, blocks_act)).reshape(EXAMPLES, FEAT)
    rounded = features.astype(jnp.bfloat16)
    gram = jnp.dot(rounded.T, rounded, preferred_element_type=jnp.float32)
    return features, gram
```

```python
import jax
import jax.numpy as jnp
from jax import lax
from jax.experimental import pallas as pl
from jax.experimental.pallas import tpu as pltpu
from jax.sharding import PartitionSpec as P

SEQ = 8
NZ, NX, NY = 8, 4, 4
GROUPS = 16
PEERS = 16
TOK = 512
TILE = 128
OWN = 32
VOC = 2000
WIDTH = 320
K = 64
EX = 4
ROWS = 64
BLK = 256
MESH = pl.DeviceIdType.MESH
F32, BF16 = jnp.float32, jnp.bfloat16


def kernel(
    logits_h, labels_h, act_h, pin_h, pout_h,
    feat_h, gram_h,
    logits, labels, act, pin, pout,
    rhs, rhs_in, labcol, left, lhs, stats,
    psend, precv, lr, feat, pieces, row_in, col_in, rows, cols, acc, xrecv, gout,
    load_sem, rs_send, rs_recv, a2a_send, a2a_recv, ag_send, row_sem, col_sem, x_send, x_recv, out_sem,
):
    d, f = lax.axis_index("dp"), lax.axis_index("fsdp")
    core, c = lax.rem(d, 2), lax.div(d, 2)
    z, yh = lax.div(c, 2), lax.rem(c, 2)
    yl, x = lax.div(f, NX), lax.rem(f, NX)

    def dev(group, peer):
        return (group * 2 + core, peer)

    loads = []
    for k, (src, dst) in enumerate(((labels_h, labels), (pout_h, pout), (pin_h, pin), (act_h, act))):
        loads.append(pltpu.make_async_copy(src, dst, load_sem.at[k]))
    quarter = [lax.rem(yl + 1 + s, NY) for s in range(NY)]
    chunks = []
    for s in range(NY):
        at = pl.ds(pl.multiple_of(quarter[s] * TILE, TILE), TILE)
        chunks.append(pltpu.make_async_copy(logits_h.at[at], logits.at[at], load_sem.at[4 + s]))
    for copy in (loads[0], loads[1], chunks[0], loads[2], loads[3], *chunks[1:]):
        copy.start()

    barrier = pltpu.get_barrier_semaphore()

    def tell(group, peer):
        pl.semaphore_signal(barrier, inc=1, device_id=dev(group, peer), device_id_type=MESH)

    z_up, z_down = lax.rem(z + 1, NZ) * 2 + yh, lax.rem(z + NZ - 1, NZ) * 2 + yh
    y_far = z * 2 + 1 - yh
    for k in range(1, PEERS):
        tell(c, lax.rem(f + k, PEERS))
    for k in range(1, PEERS):
        tell(f, lax.rem(f + k, PEERS))

    @pl.when(c != f)
    def _():
        tell(f, f)

    tell(z_up, f)
    tell(z_down, f)
    tell(y_far, f)
    other = 1 - core
    partner = (c * 2 + other, f)
    pl.semaphore_signal(barrier, inc=1, device_id=partner, device_id_type=MESH)

    lane = lax.broadcasted_iota(jnp.int32, (1, 128), 1)

    loads[0].wait()
    for q in range(NY):
        labcol[q * TILE : (q + 1) * TILE, :] = jnp.transpose(
            jnp.broadcast_to(labels[q : q + 1, :], (8, 128))
        )[:, 0:1] - f * VOC
    loads[1].wait()
    rhs[:, 0:K] = pout[...]
    rhs[:, K:128] = jnp.ones((VOC, 128 - K), BF16)

    def local_tile(s):
        q = quarter[s]
        chunks[s].wait()

        @pl.loop(0, TILE // 16)
        def _(r):
            at = pl.multiple_of(r * 16, 16)
            start = pl.multiple_of(q * TILE + at, 16)
            value = logits[pl.ds(start, 16), :].astype(F32)
            top = jnp.max(value, axis=1, keepdims=True)
            column = lax.broadcasted_iota(jnp.int32, (16, VOC), 1)
            hot = column == labcol[pl.ds(start, 16), :]
            expo = jnp.exp(value - top)
            lhs[pl.ds(at, 16), :] = jnp.where(hot, 0.0, expo).astype(BF16)
            lhs[pl.ds(TILE + at, 16), :] = jnp.where(hot, 1.0, 0.0).astype(BF16)
            at_label = jnp.sum(jnp.where(hot, value, 0.0), axis=1, keepdims=True)
            stats[pl.ds(at, 16), :] = jnp.where(lane < 112, top, at_label)

        both = jnp.dot(lhs[...], rhs[...], preferred_element_type=F32)
        a, b = both[:TILE], both[TILE:]
        low = a - a.astype(BF16).astype(F32)
        a = jnp.where(lane < 80, a, jnp.where(lane < 96, low, stats[...]))
        b = jnp.where(lane < K, b, left[pl.ds(pl.multiple_of(q * TILE, TILE), TILE), :])
        for t in range(NX):
            at = slice(t * OWN, (t + 1) * OWN)
            psend[q * NX + t, :, 0:128] = a[at].astype(BF16)
            psend[q * NX + t, :, 128:256] = b[at].astype(BF16)

    def send_share(peer):
        pltpu.make_async_remote_copy(
            src_ref=psend.at[peer], dst_ref=precv.at[f], send_sem=rs_send, recv_sem=rs_recv,
            device_id=dev(c, peer), device_id_type=MESH,
        ).start()

    for s in range(NY):
        if s == 0:
            loads[2].wait()
            loads[3].wait()
            rhs_in[:, 0:K] = jnp.zeros((WIDTH, K), BF16)
            rhs_in[:, K:128] = pin[...]
            left[...] = jnp.dot(act[...], rhs_in[...], preferred_element_type=F32)
        local_tile(s)
        if s == 0:
            @pl.when(c != f)
            def _():
                pl.semaphore_wait(barrier, 35)

            @pl.when(c == f)
            def _():
                pl.semaphore_wait(barrier, 34)

        for t in range(1, NX + 1):
            across = lax.rem(x + t, NX)
            if s < NY - 1 or t < NX:
                send_share(quarter[s] * NX + across)
    precv[f] = psend[f]

    def wait_bytes(ref, sem):
        pltpu.make_async_copy(ref, ref, sem).wait()

    wait_bytes(precv.at[pl.ds(0, PEERS - 1)], rs_recv)

    top = precv[0, :, 0:128].astype(F32)
    for k in range(1, PEERS):
        top = jnp.maximum(top, precv[k, :, 0:128].astype(F32))
    top = top[:, 96:97]
    sum_a = jnp.zeros((OWN, 128), F32)
    sum_x = jnp.zeros((OWN, 128), F32)
    sum_b = jnp.zeros((OWN, 128), F32)
    for k in range(PEERS):
        a = precv[k, :, 0:128].astype(F32)
        sum_a += jnp.exp(a[:, 96:97] - top) * a
        sum_x += a
        sum_b += precv[k, :, 128:256].astype(F32)
    rest = sum_a[:, 64:65] + sum_a[:, 80:81]
    total = rest + jnp.exp(sum_x[:, 112:113] - top)
    right = (sum_a - rest * sum_b) / total
    lr[...] = jnp.where(lane < K, right, sum_b)

    halves = []
    for s in range(SEQ // 2):
        both = jnp.concatenate(
            [lr[pl.ds(2 * s, EX, stride=SEQ), :], lr[pl.ds(2 * s + 1, EX, stride=SEQ), :]], axis=0
        )
        halves.append((both, jnp.where(lane < K, both, pltpu.roll(both, K, 1))))
    for k in range(K // 2):
        value = jnp.zeros((8, 128), F32)
        for both, wide in halves:
            first, second = both[:, K + 2 * k : K + 2 * k + 1], both[:, K + 2 * k + 1 : K + 2 * k + 2]
            value += jnp.where(lane < K, first, second) * wide
        value = value[0:EX] + value[EX:8]
        feat[:, k * 128 : (k + 1) * 128] = value
        pieces[k // 2, :, (k % 2) * 128 : (k % 2 + 1) * 128] = value.astype(BF16)
    feat_out = pltpu.make_async_copy(feat, feat_h, out_sem.at[0])
    feat_out.start()

    for k in range(1, PEERS):
        block = lax.rem(f + k, PEERS)
        pltpu.make_async_remote_copy(
            src_ref=pieces.at[block], dst_ref=row_in.at[f], send_sem=a2a_send.at[0], recv_sem=a2a_recv.at[0],
            device_id=dev(c, block), device_id_type=MESH,
        ).start()

    def send_col(block):
        pltpu.make_async_remote_copy(
            src_ref=pieces.at[block], dst_ref=col_in.at[f], send_sem=a2a_send.at[1], recv_sem=a2a_recv.at[1],
            device_id=dev(block, c), device_id_type=MESH,
        ).start()

    for k in range(1, PEERS):
        send_col(lax.rem(c + k, PEERS))

    @pl.when(c != f)
    def _():
        send_col(c)

    @pl.when(c == f)
    def _():
        col_in[f] = pieces[c]

    row_in[f] = pieces[f]
    wait_bytes(psend.at[pl.ds(0, PEERS - 1)], rs_send)

    def packed(ref):
        lines = [ref[k].astype(F32) for k in range(PEERS)]
        return jnp.concatenate(lines, axis=0).astype(BF16)

    def copy_row(chunk, target, slot):
        return pltpu.make_async_remote_copy(
            src_ref=rows.at[chunk], dst_ref=rows.at[chunk], send_sem=ag_send.at[0], recv_sem=row_sem.at[slot],
            device_id=dev(target, f), device_id_type=MESH,
        )

    def copy_col(chunk, target, slot):
        return pltpu.make_async_remote_copy(
            src_ref=cols.at[chunk], dst_ref=cols.at[chunk], send_sem=ag_send.at[1], recv_sem=col_sem.at[slot],
            device_id=dev(c, target), device_id_type=MESH,
        )

    def row_chunk(away, far):
        return lax.rem(z + NZ + away, NZ) * 2 + (1 - yh if far else yh)

    def send_row(away, far, up, slot):
        copy_row(row_chunk(away, far), z_up if up else z_down, slot).start()

    def got_row(away, far, slot):
        copy_row(row_chunk(away, far), z_up, slot).wait_recv()

    x_up, x_down = lax.rem(x + 1, NX), lax.rem(x + NX - 1, NX)
    x_two = lax.rem(x + 2, NX)

    def col_chunk(k, across):
        return lax.rem(yl + k, NY) * NX + across

    wait_bytes(row_in.at[pl.ds(0, PEERS - 1)], a2a_recv.at[0])
    rows[c] = packed(row_in)
    send_row(0, False, True, 0)
    send_row(0, False, False, 4)
    copy_row(c, y_far, 14).start()

    @pl.when(c != f)
    def _():
        wait_bytes(col_in, a2a_recv.at[1])

    @pl.when(c == f)
    def _():
        wait_bytes(col_in.at[pl.ds(0, PEERS - 1)], a2a_recv.at[1])

    cols[f] = packed(col_in)
    for k in range(1, NY):
        copy_col(f, lax.rem(yl + k, NY) * NX + x, NY - 1 - k).start()

    def col_send(k):
        copy_col(col_chunk(k, x), yl * NX + x_up, 3 + 3 * k).start()
        copy_col(col_chunk(k, x), yl * NX + x_down, 4 + 3 * k).start()

    def col_pass(k):
        copy_col(col_chunk(k, x_down), yl * NX + x_up, 3 + 3 * k).wait_recv()
        if k % 2 == 0:
            copy_col(col_chunk(k, x_down), yl * NX + x_up, 5 + 3 * k).start()
        copy_col(col_chunk(k, x_up), yl * NX + x_up, 4 + 3 * k).wait_recv()
        if k % 2 == 1:
            copy_col(col_chunk(k, x_up), yl * NX + x_down, 5 + 3 * k).start()

    col_send(0)
    wait_bytes(pieces.at[pl.ds(0, PEERS - 1)], a2a_send.at[0])

    @pl.when(c != f)
    def _():
        wait_bytes(pieces, a2a_send.at[1])

    @pl.when(c == f)
    def _():
        wait_bytes(pieces.at[pl.ds(0, PEERS - 1)], a2a_send.at[1])

    got_row(-1, False, 0)
    send_row(-1, False, True, 1)
    got_row(1, False, 4)
    send_row(1, False, False, 5)
    for k in range(1, NY):
        copy_col(col_chunk(k, x), f, k - 1).wait_recv()
        col_send(k)
    copy_row(y_far, y_far, 14).wait_recv()
    send_row(0, True, True, 7)
    send_row(0, True, False, 10)
    col_pass(0)
    got_row(-2, False, 1)
    send_row(-2, False, True, 2)
    got_row(2, False, 5)
    send_row(2, False, False, 6)
    got_row(-1, True, 7)
    send_row(-1, True, True, 8)
    got_row(1, True, 10)
    send_row(1, True, False, 11)
    for k in range(1, NY):
        col_pass(k)
    got_row(-3, False, 2)
    send_row(-3, False, True, 3)
    got_row(-2, True, 8)
    send_row(-2, True, True, 9)
    got_row(2, True, 11)
    send_row(2, True, False, 12)
    for k in range(NY):
        copy_col(col_chunk(k, x_two), f, 5 + 3 * k).wait_recv()

    def product(away):
        at = pl.ds(lax.rem(z + NZ + away, NZ) * 2, 2)
        a = rows[at].reshape(2 * ROWS, BLK)
        b = cols[at].reshape(2 * ROWS, BLK)
        return lax.dot_general(a, b, (((0,), (0,)), ((), ())), preferred_element_type=F32)

    def add(away):
        value = product(away)
        acc[0] += value[:, 0:128]
        acc[1] += value[:, 128:256]

    value = product(0)
    acc[0] = value[:, 0:128]
    acc[1] = value[:, 128:256]
    got_row(3, True, 12)
    send_row(3, True, False, 13)
    for away in (-1, 1, -2, 2):
        add(away)
    got_row(-3, True, 9)
    add(-3)
    got_row(3, False, 6)
    add(3)
    got_row(-4, False, 3)
    got_row(-4, True, 13)
    add(-4)

    swap = pltpu.make_async_remote_copy(
        src_ref=acc.at[other], dst_ref=xrecv, send_sem=x_send, recv_sem=x_recv,
        device_id=partner, device_id_type=MESH,
    )
    swap.start()
    wait_bytes(rows.at[pl.ds(0, GROUPS - 1)], ag_send.at[0])
    wait_bytes(cols.at[pl.ds(0, PEERS - 1)], ag_send.at[1])
    feat_out.wait()
    swap.wait_recv()
    gout[...] = acc[core] + xrecv[...]
    gram_out = pltpu.make_async_copy(gout, gram_h, out_sem.at[1])
    gram_out.start()
    swap.wait_send()
    gram_out.wait()


def body(logits, labels, activations, proj_in, proj_out):
    dma, vmem = pltpu.SemaphoreType.DMA, pltpu.VMEM
    return pl.pallas_call(
        kernel,
        out_shape=(
            jax.ShapeDtypeStruct((EX, K * K), F32),
            jax.ShapeDtypeStruct((BLK, BLK // 2), F32),
        ),
        in_specs=[pl.BlockSpec(memory_space=pl.ANY)] * 5,
        out_specs=(pl.BlockSpec(memory_space=pl.ANY),) * 2,
        scratch_shapes=[
            vmem((TOK, VOC), BF16),
            vmem((NY, TILE), jnp.int32),
            vmem((TOK, WIDTH), BF16),
            vmem((WIDTH, K), BF16),
            vmem((VOC, K), BF16),
            vmem((VOC, 128), BF16),
            vmem((WIDTH, 128), BF16),
            vmem((TOK, 1), jnp.int32),
            vmem((TOK, 128), F32),
            vmem((2 * TILE, VOC), BF16),
            vmem((TILE, 128), F32),
            vmem((PEERS, OWN, 256), BF16),
            vmem((PEERS, OWN, 256), BF16),
            vmem((OWN, 128), F32),
            vmem((EX, K * K), F32),
            vmem((PEERS, EX, BLK), BF16),
            vmem((PEERS, EX, BLK), BF16),
            vmem((PEERS, EX, BLK), BF16),
            vmem((GROUPS, ROWS, BLK), BF16),
            vmem((PEERS, ROWS, BLK), BF16),
            vmem((2, BLK, 128), F32),
            vmem((BLK, 128), F32),
            vmem((BLK, 128), F32),
            dma((4 + NY,)),
            dma, dma,
            dma((2,)), dma((2,)),
            dma((2,)), dma((15,)), dma((15,)),
            dma, dma,
            dma((2,)),
        ],
        compiler_params=pltpu.CompilerParams(
            collective_id=0, has_side_effects=True, vmem_limit_bytes=40 * 1024 * 1024
        ),
        cost_estimate=pl.CostEstimate(flops=500_000_000, bytes_accessed=4_000_000, transcendentals=1_100_000),
    )(logits, labels.reshape(NY, TILE), activations, proj_in, proj_out)


def solution(mesh):
    in_specs = (P("dp", "fsdp"), P("dp"), P("dp", "fsdp"), P("fsdp", None), P("fsdp", None))
    out_specs = (P(("dp", "fsdp"), None), P("fsdp", "dp"))
    return jax.shard_map(body, mesh=mesh, in_specs=in_specs, out_specs=out_specs, check_vma=False)
```

```python
import jax
import jax.numpy as jnp
from jax import lax
from jax.experimental import pallas as pl
from jax.experimental.pallas import tpu as pltpu
from jax.sharding import PartitionSpec as P

SEQ = 8
NZ, NX, NY = 8, 4, 4
GROUPS = 16
PEERS = 16
TOK = 512
TILE = 128
OWN = 32
VOC = 2000
WIDTH = 320
K = 64
EX = 4
ROWS = 64
BLK = 256
MESH = pl.DeviceIdType.MESH
F32, BF16 = jnp.float32, jnp.bfloat16


def kernel(
    logits_h, labels_h, act_h, pin_h, pout_h,
    feat_h, gram_h,
    logits, labels, act, pin, weights, left,
    psend, precv, lr, feat, pieces, row_in, col_in, rows, cols, acc, xrecv, gout,
    load_sem, rs_send, rs_recv, a2a_send, a2a_recv, ag_send, row_sem, col_sem, x_send, x_recv, out_sem,
):
    d, f = lax.axis_index("dp"), lax.axis_index("fsdp")
    core, c = lax.rem(d, 2), lax.div(d, 2)
    z, yh = lax.div(c, 2), lax.rem(c, 2)
    yl, x = lax.div(f, NX), lax.rem(f, NX)

    def dev(group, peer):
        return (group * 2 + core, peer)

    quarter = [lax.rem(yl + 1 + s, NY) for s in range(NY)]
    chunks = []
    for s in range(NY):
        at = pl.ds(pl.multiple_of(quarter[s] * TILE, TILE), TILE)
        chunks.append(pltpu.make_async_copy(logits_h.at[:, at], logits.at[s], load_sem.at[4 + s]))
    pairs = ((labels_h, labels), (pout_h, weights.at[0:K]), (pin_h, pin), (act_h, act))
    loads = [pltpu.make_async_copy(src, dst, load_sem.at[k]) for k, (src, dst) in enumerate(pairs)]
    for copy in (chunks[0], loads[0], loads[1], chunks[1], loads[2], loads[3], *chunks[2:]):
        copy.start()

    barrier = pltpu.get_barrier_semaphore()

    def tell(group, peer):
        pl.semaphore_signal(barrier, inc=1, device_id=dev(group, peer), device_id_type=MESH)

    def away(k):
        return lax.rem(z + NZ + k, NZ)

    y_far = z * 2 + 1 - yh
    for k in range(1, PEERS):
        tell(c, lax.rem(f + k, PEERS))
    for k in range(1, PEERS):
        tell(f, lax.rem(f + k, PEERS))

    @pl.when(c != f)
    def _():
        tell(f, f)

    for k in range(PEERS):
        tell(y_far, lax.rem(f + k, PEERS))
    for k in (-2, -1, 1, 2):
        tell(away(k) * 2 + yh, f)
    other = 1 - core
    partner = (c * 2 + other, f)
    pl.semaphore_signal(barrier, inc=1, device_id=partner, device_id_type=MESH)

    lane = lax.broadcasted_iota(jnp.int32, (1, 128), 1)

    weights[K : K + 16, :] = jnp.ones((16, VOC), BF16)

    def local_tile(s):
        q = quarter[s]
        chunks[s].wait()
        top = logits[s, 0:80, :]
        for at in range(80, VOC, 80):
            top = jnp.maximum(top, logits[s, at : at + 80, :])
        top = jnp.max(top.astype(F32), axis=0, keepdims=True)
        if s == 0:
            loads[0].wait()
            loads[1].wait()
        token = labels[pl.ds(q, 1), :] - f * VOC
        both = jnp.zeros((K + 16, 2 * TILE), F32)
        at_label = jnp.zeros((8, TILE), F32)
        for at in range(0, VOC, 256):
            size = min(256, VOC - at)
            value = logits[s, at : at + size, :].astype(F32)
            hot = lax.broadcasted_iota(jnp.int32, (size, TILE), 0) == token - at
            expo = jnp.where(hot, 0.0, jnp.exp(value - top)).astype(BF16)
            ones = jnp.where(hot, 1.0, 0.0).astype(BF16)
            at_label += jnp.sum(jnp.where(hot, value, 0.0).reshape(size // 8, 8, TILE), axis=0)
            both += jnp.dot(
                weights[:, at : at + size], jnp.concatenate([expo, ones], axis=1), preferred_element_type=F32
            )
        at_label = jnp.sum(at_label, axis=0, keepdims=True)
        total = both[K : K + 16, :TILE]
        low = total - total.astype(BF16).astype(F32)
        wide = (16, TILE)
        a = jnp.concatenate(
            [both[:K, :TILE], total, low, jnp.broadcast_to(top, wide), jnp.broadcast_to(at_label, wide)], axis=0
        )
        b = jnp.concatenate([both[:K, TILE:], left[q]], axis=0)
        a, b = a.T, b.T
        for t in range(NX):
            at = slice(t * OWN, (t + 1) * OWN)
            psend[q * NX + t, :, 0:128] = a[at].astype(BF16)
            psend[q * NX + t, :, 128:256] = b[at].astype(BF16)

    def send_share(peer):
        pltpu.make_async_remote_copy(
            src_ref=psend.at[peer], dst_ref=precv.at[f], send_sem=rs_send, recv_sem=rs_recv,
            device_id=dev(c, peer), device_id_type=MESH,
        ).start()

    for s in range(NY):
        if s == 0:
            loads[2].wait()
            loads[3].wait()
            both = jnp.dot(pin[...], act[...], preferred_element_type=F32)
            for q in range(NY):
                left[q] = both[:, q * TILE : (q + 1) * TILE]
        local_tile(s)
        if s == 0:
            @pl.when(c != f)
            def _():
                pl.semaphore_wait(barrier, 52)

            @pl.when(c == f)
            def _():
                pl.semaphore_wait(barrier, 51)

        for t in range(1, NX + 1):
            across = lax.rem(x + t, NX)
            if s < NY - 1 or t < NX:
                send_share(quarter[s] * NX + across)
    precv[f] = psend[f]

    def wait_bytes(ref, sem):
        pltpu.make_async_copy(ref, ref, sem).wait()

    wait_bytes(precv.at[pl.ds(0, PEERS - 1)], rs_recv)

    top = precv[0, :, 0:128].astype(F32)
    for k in range(1, PEERS):
        top = jnp.maximum(top, precv[k, :, 0:128].astype(F32))
    top = top[:, 96:97]
    sum_a = jnp.zeros((OWN, 128), F32)
    sum_x = jnp.zeros((OWN, 128), F32)
    sum_b = jnp.zeros((OWN, 128), F32)
    for k in range(PEERS):
        a = precv[k, :, 0:128].astype(F32)
        sum_a += jnp.exp(a[:, 96:97] - top) * a
        sum_x += a
        sum_b += precv[k, :, 128:256].astype(F32)
    rest = sum_a[:, 64:65] + sum_a[:, 80:81]
    total = rest + jnp.exp(sum_x[:, 112:113] - top)
    right = (sum_a - rest * sum_b) / total
    lr[...] = jnp.where(lane < K, right, sum_b)

    halves = []
    for s in range(SEQ // 2):
        both = jnp.concatenate(
            [lr[pl.ds(2 * s, EX, stride=SEQ), :], lr[pl.ds(2 * s + 1, EX, stride=SEQ), :]], axis=0
        )
        halves.append((both, jnp.where(lane < K, both, pltpu.roll(both, K, 1))))
    for k in range(K // 2):
        value = jnp.zeros((8, 128), F32)
        for both, wide in halves:
            first, second = both[:, K + 2 * k : K + 2 * k + 1], both[:, K + 2 * k + 1 : K + 2 * k + 2]
            value += jnp.where(lane < K, first, second) * wide
        value = value[0:EX] + value[EX:8]
        feat[:, k * 128 : (k + 1) * 128] = value
        pieces[k // 2, :, (k % 2) * 128 : (k % 2 + 1) * 128] = value.astype(BF16)
    feat_out = pltpu.make_async_copy(feat, feat_h, out_sem.at[0])
    feat_out.start()

    def send_row(group, block):
        pltpu.make_async_remote_copy(
            src_ref=pieces.at[block], dst_ref=row_in.at[yh * PEERS + f], send_sem=a2a_send.at[0],
            recv_sem=a2a_recv.at[0], device_id=dev(group, block), device_id_type=MESH,
        ).start()

    for k in range(1, PEERS):
        send_row(y_far, lax.rem(f + k, PEERS))
        send_row(c, lax.rem(f + k, PEERS))
    send_row(y_far, f)

    def send_col(block):
        pltpu.make_async_remote_copy(
            src_ref=pieces.at[block], dst_ref=col_in.at[f], send_sem=a2a_send.at[1], recv_sem=a2a_recv.at[1],
            device_id=dev(block, c), device_id_type=MESH,
        ).start()

    for k in range(1, PEERS):
        send_col(lax.rem(c + k, PEERS))

    @pl.when(c != f)
    def _():
        send_col(c)

    @pl.when(c == f)
    def _():
        col_in[f] = pieces[c]

    row_in[yh * PEERS + f] = pieces[f]
    wait_bytes(psend.at[pl.ds(0, PEERS - 1)], rs_send)

    def packed(ref, first):
        lines = [ref[first + k].astype(F32) for k in range(PEERS)]
        return jnp.concatenate(lines, axis=0).astype(BF16)

    def copy_row(origin, half, target, up, hops):
        at = pl.ds(half * ROWS, ROWS)
        ref = rows.at[away(origin), at]
        return pltpu.make_async_remote_copy(
            src_ref=ref, dst_ref=ref, send_sem=ag_send.at[0], recv_sem=row_sem.at[(half * 2 + up) * 4 + hops - 1],
            device_id=dev(away(target) * 2 + yh, f), device_id_type=MESH,
        )

    def copy_col(chunk, target, slot):
        return pltpu.make_async_remote_copy(
            src_ref=cols.at[chunk], dst_ref=cols.at[chunk], send_sem=ag_send.at[1], recv_sem=col_sem.at[slot],
            device_id=dev(c, target), device_id_type=MESH,
        )

    x_up, x_down = lax.rem(x + 1, NX), lax.rem(x + NX - 1, NX)
    x_two = lax.rem(x + 2, NX)

    def col_chunk(k, across):
        return lax.rem(yl + k, NY) * NX + across

    wait_bytes(row_in.at[pl.ds(0, 2 * PEERS - 1)], a2a_recv.at[0])
    for half in range(2):
        rows[z, half * ROWS : (half + 1) * ROWS, :] = packed(row_in, half * PEERS)
    for hops in (2, 1):
        for half in range(2):
            copy_row(0, half, hops, 1, hops).start()
            copy_row(0, half, -hops, 0, hops).start()

    @pl.when(c != f)
    def _():
        wait_bytes(col_in, a2a_recv.at[1])

    @pl.when(c == f)
    def _():
        wait_bytes(col_in.at[pl.ds(0, PEERS - 1)], a2a_recv.at[1])

    cols[f] = packed(col_in, 0)
    for k in range(1, NY):
        copy_col(f, lax.rem(yl + k, NY) * NX + x, NY - 1 - k).start()

    def col_send(k):
        copy_col(col_chunk(k, x), yl * NX + x_up, 3 + 3 * k).start()
        copy_col(col_chunk(k, x), yl * NX + x_down, 4 + 3 * k).start()

    def col_pass(k):
        copy_col(col_chunk(k, x_down), yl * NX + x_up, 3 + 3 * k).wait_recv()
        if k % 2 == 0:
            copy_col(col_chunk(k, x_down), yl * NX + x_up, 5 + 3 * k).start()
        copy_col(col_chunk(k, x_up), yl * NX + x_up, 4 + 3 * k).wait_recv()
        if k % 2 == 1:
            copy_col(col_chunk(k, x_up), yl * NX + x_down, 5 + 3 * k).start()

    col_send(0)
    wait_bytes(row_in.at[pl.ds(0, 2 * PEERS - 1)], a2a_send.at[0])

    @pl.when(c != f)
    def _():
        wait_bytes(pieces, a2a_send.at[1])

    @pl.when(c == f)
    def _():
        wait_bytes(pieces.at[pl.ds(0, PEERS - 1)], a2a_send.at[1])

    for half in range(2):
        for up, sign in ((1, 1), (0, -1)):
            copy_row(-2 * sign, half, 1, up, 2).wait_recv()
            if up != half:
                copy_row(-2 * sign, half, 2 * sign, up, 4).start()
            copy_row(-2 * sign, half, sign, up, 3).start()
    for k in range(1, NY):
        copy_col(col_chunk(k, x), f, k - 1).wait_recv()
        col_send(k)
    for k in range(NY):
        col_pass(k)
    for k in range(NY):
        copy_col(col_chunk(k, x_two), f, 5 + 3 * k).wait_recv()

    def product(k):
        at = away(k)
        b = cols[pl.ds(at * 2, 2)].reshape(2 * ROWS, BLK)
        return lax.dot_general(rows[at], b, (((0,), (0,)), ((), ())), preferred_element_type=F32)

    total = product(0)
    for hops in (2, 1, 3):
        for up, sign in ((1, 1), (0, -1)):
            for half in range(2):
                if hops != 2:
                    copy_row(-hops * sign, half, 1, up, hops).wait_recv()
            total += product(-hops * sign)
    copy_row(-4, 0, 1, 1, 4).wait_recv()
    copy_row(-4, 1, 1, 0, 4).wait_recv()
    total += product(-4)
    acc[0] = total[:, 0:128]
    acc[1] = total[:, 128:256]

    swap = pltpu.make_async_remote_copy(
        src_ref=acc.at[other], dst_ref=xrecv, send_sem=x_send, recv_sem=x_recv,
        device_id=partner, device_id_type=MESH,
    )
    swap.start()
    wait_bytes(rows.at[pl.ds(0, NZ - 1)], ag_send.at[0])
    wait_bytes(cols.at[pl.ds(0, PEERS - 1)], ag_send.at[1])
    feat_out.wait()
    swap.wait_recv()
    gout[...] = acc[core] + xrecv[...]
    gram_out = pltpu.make_async_copy(gout, gram_h, out_sem.at[1])
    gram_out.start()
    swap.wait_send()
    gram_out.wait()


def body(logits, labels, activations, proj_in, proj_out):
    dma, vmem = pltpu.SemaphoreType.DMA, pltpu.VMEM
    return pl.pallas_call(
        kernel,
        out_shape=(
            jax.ShapeDtypeStruct((EX, K * K), F32),
            jax.ShapeDtypeStruct((BLK, BLK // 2), F32),
        ),
        in_specs=[pl.BlockSpec(memory_space=pltpu.HBM)] * 5,
        out_specs=(pl.BlockSpec(memory_space=pltpu.HBM),) * 2,
        scratch_shapes=[
            vmem((NY, VOC, TILE), BF16),
            vmem((NY, TILE), jnp.int32),
            vmem((WIDTH, TOK), BF16),
            vmem((K, WIDTH), BF16),
            vmem((K + 16, VOC), BF16),
            vmem((NY, K, TILE), F32),
            vmem((PEERS, OWN, 256), BF16),
            vmem((PEERS, OWN, 256), BF16),
            vmem((OWN, 128), F32),
            vmem((EX, K * K), F32),
            vmem((PEERS, EX, BLK), BF16),
            vmem((2 * PEERS, EX, BLK), BF16),
            vmem((PEERS, EX, BLK), BF16),
            vmem((NZ, 2 * ROWS, BLK), BF16),
            vmem((PEERS, ROWS, BLK), BF16),
            vmem((2, BLK, 128), F32),
            vmem((BLK, 128), F32),
            vmem((BLK, 128), F32),
            dma((4 + NY,)),
            dma, dma,
            dma((2,)), dma((2,)),
            dma((2,)), dma((16,)), dma((15,)),
            dma, dma,
            dma((2,)),
        ],
        compiler_params=pltpu.CompilerParams(
            collective_id=0, has_side_effects=True, vmem_limit_bytes=58 * 1024 * 1024
        ),
        cost_estimate=pl.CostEstimate(flops=500_000_000, bytes_accessed=4_000_000, transcendentals=1_100_000),
    )(logits.T, labels.reshape(NY, TILE), activations.T, proj_in.T, proj_out.T)


def solution(mesh):
    in_specs = (P("dp", "fsdp"), P("dp"), P("dp", "fsdp"), P("fsdp", None), P("fsdp", None))
    out_specs = (P(("dp", "fsdp"), None), P("fsdp", "dp"))
    return jax.shard_map(body, mesh=mesh, in_specs=in_specs, out_specs=out_specs, check_vma=False)
```

```python
import jax
import jax.numpy as jnp
from jax import lax
from jax.experimental import pallas as pl
from jax.experimental.pallas import tpu as pltpu
from jax.sharding import PartitionSpec as P

SEQ = 8
NZ, NX, NY = 8, 4, 4
GROUPS = 16
PEERS = 16
TOK = 512
TILE = 128
OWN = 32
VOC = 2000
WIDTH = 320
K = 64
EX = 4
ROWS = 64
BLK = 256
MESH = pl.DeviceIdType.MESH
F32, BF16 = jnp.float32, jnp.bfloat16


def kernel(
    logits_h, labels_h, act_h, pin_h, pout_h,
    feat_h, gram_h,
    logits, labels, act, pin, weights, left,
    psend, precv, lr, feat, pieces, row_in, col_in, rows, cols, acc, xrecv, gout,
    load_sem, rs_send, rs_recv, a2a_send, a2a_recv, ag_send, row_sem, col_sem, x_send, x_recv, out_sem,
):
    d, f = lax.axis_index("dp"), lax.axis_index("fsdp")
    core, c = lax.rem(d, 2), lax.div(d, 2)
    z, yh = lax.div(c, 2), lax.rem(c, 2)
    yl, x = lax.div(f, NX), lax.rem(f, NX)

    def dev(group, peer):
        return (group * 2 + core, peer)

    quarter = [lax.rem(yl + 1 + s, NY) for s in range(NY)]
    chunks = []
    for s in range(NY):
        at = pl.ds(pl.multiple_of(quarter[s] * TILE, TILE), TILE)
        chunks.append(pltpu.make_async_copy(logits_h.at[:, at], logits.at[s], load_sem.at[4 + s]))
    pairs = ((labels_h, labels), (pout_h, weights.at[0:K]), (pin_h, pin), (act_h, act))
    loads = [pltpu.make_async_copy(src, dst, load_sem.at[k]) for k, (src, dst) in enumerate(pairs)]
    for copy in (chunks[0], loads[0], loads[1], chunks[1], loads[2], loads[3], *chunks[2:]):
        copy.start()

    barrier = pltpu.get_barrier_semaphore()

    def tell(group, peer):
        pl.semaphore_signal(barrier, inc=1, device_id=dev(group, peer), device_id_type=MESH)

    def away(k):
        return lax.rem(z + NZ + k, NZ)

    y_far = z * 2 + 1 - yh
    for k in range(1, PEERS):
        tell(c, lax.rem(f + k, PEERS))

    @pl.when(c != f)
    def _():
        tell(f, c)

    tell(y_far, f)
    for k in (-2, -1, 1, 2):
        tell(away(k) * 2 + yh, f)
    other = 1 - core
    partner = (c * 2 + other, f)
    pl.semaphore_signal(barrier, inc=1, device_id=partner, device_id_type=MESH)

    lane = lax.broadcasted_iota(jnp.int32, (1, 128), 1)

    weights[K : K + 16, :] = jnp.ones((16, VOC), BF16)

    def local_tile(s):
        q = quarter[s]
        chunks[s].wait()
        top = logits[s, 0:80, :]
        for at in range(80, VOC, 80):
            top = jnp.maximum(top, logits[s, at : at + 80, :])
        top = jnp.max(top.astype(F32), axis=0, keepdims=True)
        if s == 0:
            loads[0].wait()
            loads[1].wait()
        token = labels[pl.ds(q, 1), :] - f * VOC
        both = jnp.zeros((K + 16, 2 * TILE), F32)
        at_label = jnp.zeros((8, TILE), F32)
        for at in range(0, VOC, 256):
            size = min(256, VOC - at)
            value = logits[s, at : at + size, :].astype(F32)
            hot = lax.broadcasted_iota(jnp.int32, (size, TILE), 0) == token - at
            expo = jnp.where(hot, 0.0, jnp.exp(value - top)).astype(BF16)
            ones = jnp.where(hot, 1.0, 0.0).astype(BF16)
            at_label += jnp.sum(jnp.where(hot, value, 0.0).reshape(size // 8, 8, TILE), axis=0)
            both += jnp.dot(
                weights[:, at : at + size], jnp.concatenate([expo, ones], axis=1), preferred_element_type=F32
            )
        at_label = jnp.sum(at_label, axis=0, keepdims=True)
        total = both[K : K + 16, :TILE]
        low = total - total.astype(BF16).astype(F32)
        wide = (16, TILE)
        a = jnp.concatenate(
            [both[:K, :TILE], total, low, jnp.broadcast_to(top, wide), jnp.broadcast_to(at_label, wide)], axis=0
        )
        b = jnp.concatenate([both[:K, TILE:], left[q]], axis=0)
        a, b = a.T, b.T
        for t in range(NX):
            at = slice(t * OWN, (t + 1) * OWN)
            psend[q * NX + t, :, 0:128] = a[at].astype(BF16)
            psend[q * NX + t, :, 128:256] = b[at].astype(BF16)

    def send_share(peer):
        pltpu.make_async_remote_copy(
            src_ref=psend.at[peer], dst_ref=precv.at[f], send_sem=rs_send, recv_sem=rs_recv,
            device_id=dev(c, peer), device_id_type=MESH,
        ).start()

    for s in range(NY):
        if s == 0:
            loads[2].wait()
            loads[3].wait()
            both = jnp.dot(pin[...], act[...], preferred_element_type=F32)
            for q in range(NY):
                left[q] = both[:, q * TILE : (q + 1) * TILE]
        local_tile(s)
        if s == 0:
            @pl.when(c != f)
            def _():
                pl.semaphore_wait(barrier, 22)

            @pl.when(c == f)
            def _():
                pl.semaphore_wait(barrier, 21)

        for t in range(1, NX + 1):
            across = lax.rem(x + t, NX)
            if s < NY - 1 or t < NX:
                send_share(quarter[s] * NX + across)
    precv[f] = psend[f]

    def wait_bytes(ref, sem):
        pltpu.make_async_copy(ref, ref, sem).wait()

    wait_bytes(precv.at[pl.ds(0, PEERS - 1)], rs_recv)

    top = precv[0, :, 0:128].astype(F32)
    for k in range(1, PEERS):
        top = jnp.maximum(top, precv[k, :, 0:128].astype(F32))
    top = top[:, 96:97]
    sum_a = jnp.zeros((OWN, 128), F32)
    sum_x = jnp.zeros((OWN, 128), F32)
    sum_b = jnp.zeros((OWN, 128), F32)
    for k in range(PEERS):
        a = precv[k, :, 0:128].astype(F32)
        sum_a += jnp.exp(a[:, 96:97] - top) * a
        sum_x += a
        sum_b += precv[k, :, 128:256].astype(F32)
    rest = sum_a[:, 64:65] + sum_a[:, 80:81]
    total = rest + jnp.exp(sum_x[:, 112:113] - top)
    right = (sum_a - rest * sum_b) / total
    lr[...] = jnp.where(lane < K, right, sum_b)

    halves = []
    for s in range(SEQ // 2):
        both = jnp.concatenate(
            [lr[pl.ds(2 * s, EX, stride=SEQ), :], lr[pl.ds(2 * s + 1, EX, stride=SEQ), :]], axis=0
        )
        halves.append((both, jnp.where(lane < K, both, pltpu.roll(both, K, 1))))
    for k in range(K // 2):
        value = jnp.zeros((8, 128), F32)
        for both, wide in halves:
            first, second = both[:, K + 2 * k : K + 2 * k + 1], both[:, K + 2 * k + 1 : K + 2 * k + 2]
            value += jnp.where(lane < K, first, second) * wide
        value = value[0:EX] + value[EX:8]
        feat[:, k * 128 : (k + 1) * 128] = value
        pieces[k // 2, :, (k % 2) * 128 : (k % 2 + 1) * 128] = value.astype(BF16)
    feat_out = pltpu.make_async_copy(feat, feat_h, out_sem.at[0])
    feat_out.start()

    def send_row(group, block, far):
        pltpu.make_async_remote_copy(
            src_ref=pieces.at[block], dst_ref=row_in.at[far, f], send_sem=a2a_send.at[2 * far],
            recv_sem=a2a_recv.at[2 * far], device_id=dev(group, block), device_id_type=MESH,
        ).start()

    for k in range(1, PEERS):
        send_row(c, lax.rem(f + k, PEERS), 0)
    for k in range(PEERS):
        send_row(y_far, lax.rem(f + k, PEERS), 1)

    def send_col(block):
        pltpu.make_async_remote_copy(
            src_ref=pieces.at[block], dst_ref=col_in.at[f], send_sem=a2a_send.at[1], recv_sem=a2a_recv.at[1],
            device_id=dev(block, c), device_id_type=MESH,
        ).start()

    for k in range(1, PEERS):
        send_col(lax.rem(c + k, PEERS))

    @pl.when(c != f)
    def _():
        send_col(c)

    @pl.when(c == f)
    def _():
        col_in[f] = pieces[c]

    row_in[0, f] = pieces[f]
    wait_bytes(psend.at[pl.ds(0, PEERS - 1)], rs_send)

    def packed(ref):
        lines = [ref[k].astype(F32) for k in range(PEERS)]
        return jnp.concatenate(lines, axis=0).astype(BF16)

    sides = [pl.ds(pl.multiple_of(half * ROWS, ROWS), ROWS) for half in (yh, 1 - yh)]

    def copy_row(origin, far, target, up, hops):
        ref = rows.at[away(origin), sides[far]]
        return pltpu.make_async_remote_copy(
            src_ref=ref, dst_ref=ref, send_sem=ag_send.at[0], recv_sem=row_sem.at[(far * 2 + up) * 4 + hops - 1],
            device_id=dev(away(target) * 2 + yh, f), device_id_type=MESH,
        )

    def row_start(far):
        rows[z, sides[far], :] = packed(row_in.at[far])
        copy_row(0, far, 2, 1, 2).start()
        copy_row(0, far, -2, 0, 2).start()

    def row_pass(far):
        for up, sign in ((1, 1), (0, -1)):
            copy_row(-2 * sign, far, 1, up, 2).wait_recv()
            if up != far:
                copy_row(-2 * sign, far, 2 * sign, up, 4).start()
            copy_row(-2 * sign, far, sign, up, 3).start()

    def copy_col(chunk, target, slot):
        return pltpu.make_async_remote_copy(
            src_ref=cols.at[chunk], dst_ref=cols.at[chunk], send_sem=ag_send.at[1], recv_sem=col_sem.at[slot],
            device_id=dev(c, target), device_id_type=MESH,
        )

    x_up, x_down = lax.rem(x + 1, NX), lax.rem(x + NX - 1, NX)
    x_two = lax.rem(x + 2, NX)

    def col_chunk(k, across):
        return lax.rem(yl + k, NY) * NX + across

    wait_bytes(row_in.at[0, pl.ds(0, PEERS - 1)], a2a_recv.at[0])
    row_start(0)
    wait_bytes(row_in.at[1], a2a_recv.at[2])
    row_start(1)

    @pl.when(c != f)
    def _():
        wait_bytes(col_in, a2a_recv.at[1])

    @pl.when(c == f)
    def _():
        wait_bytes(col_in.at[pl.ds(0, PEERS - 1)], a2a_recv.at[1])

    cols[f] = packed(col_in)
    for k in range(1, NY):
        copy_col(f, lax.rem(yl + k, NY) * NX + x, NY - 1 - k).start()

    def col_send(k):
        copy_col(col_chunk(k, x), yl * NX + x_up, 3 + 3 * k).start()
        copy_col(col_chunk(k, x), yl * NX + x_down, 4 + 3 * k).start()

    def col_pass(k):
        copy_col(col_chunk(k, x_down), yl * NX + x_up, 3 + 3 * k).wait_recv()
        if k % 2 == 0:
            copy_col(col_chunk(k, x_down), yl * NX + x_up, 5 + 3 * k).start()
        copy_col(col_chunk(k, x_up), yl * NX + x_up, 4 + 3 * k).wait_recv()
        if k % 2 == 1:
            copy_col(col_chunk(k, x_up), yl * NX + x_down, 5 + 3 * k).start()

    col_send(0)
    wait_bytes(row_in.at[0, pl.ds(0, PEERS - 1)], a2a_send.at[0])
    wait_bytes(row_in.at[1], a2a_send.at[2])

    @pl.when(c != f)
    def _():
        wait_bytes(pieces, a2a_send.at[1])

    @pl.when(c == f)
    def _():
        wait_bytes(pieces.at[pl.ds(0, PEERS - 1)], a2a_send.at[1])

    for far in (0, 1):
        copy_row(0, far, 1, 1, 1).start()
        copy_row(0, far, -1, 0, 1).start()
    row_pass(0)
    for k in (1, 3, 2):
        copy_col(col_chunk(k, x), f, k - 1).wait_recv()
        col_send(k)
    col_pass(0)
    row_pass(1)
    for k in (1, 3, 2):
        col_pass(k)
    for hops in (1, 3):
        for far in (0, 1):
            for up, sign in ((1, 1), (0, -1)):
                copy_row(-hops * sign, far, 1, up, hops).wait_recv()
    copy_row(-4, 0, 1, 1, 4).wait_recv()
    copy_row(-4, 1, 1, 0, 4).wait_recv()

    def product(at):
        b = cols[pl.ds(at * 2, 2)].reshape(2 * ROWS, BLK)
        return lax.dot_general(rows[at], b, (((0,), (0,)), ((), ())), preferred_element_type=F32)

    total = jnp.zeros((BLK, BLK), F32)
    for k in (0, 1, 3, 2):
        total += product(lax.rem(yl + k, NY) * 2 + lax.div(x, 2))
    for k in (0, 1, 3, 2):
        copy_col(col_chunk(k, x_two), f, 5 + 3 * k).wait_recv()
        total += product(lax.rem(yl + k, NY) * 2 + 1 - lax.div(x, 2))
    acc[0] = total[:, 0:128]
    acc[1] = total[:, 128:256]

    swap = pltpu.make_async_remote_copy(
        src_ref=acc.at[other], dst_ref=xrecv, send_sem=x_send, recv_sem=x_recv,
        device_id=partner, device_id_type=MESH,
    )
    swap.start()
    wait_bytes(rows.at[pl.ds(0, NZ - 1)], ag_send.at[0])
    wait_bytes(cols.at[pl.ds(0, PEERS - 1)], ag_send.at[1])
    feat_out.wait()
    swap.wait_recv()
    gout[...] = acc[core] + xrecv[...]
    gram_out = pltpu.make_async_copy(gout, gram_h, out_sem.at[1])
    gram_out.start()
    swap.wait_send()
    gram_out.wait()


def body(logits, labels, activations, proj_in, proj_out):
    dma, vmem = pltpu.SemaphoreType.DMA, pltpu.VMEM
    return pl.pallas_call(
        kernel,
        out_shape=(
            jax.ShapeDtypeStruct((EX, K * K), F32),
            jax.ShapeDtypeStruct((BLK, BLK // 2), F32),
        ),
        in_specs=[pl.BlockSpec(memory_space=pltpu.HBM)] * 5,
        out_specs=(pl.BlockSpec(memory_space=pltpu.HBM),) * 2,
        scratch_shapes=[
            vmem((NY, VOC, TILE), BF16),
            vmem((NY, TILE), jnp.int32),
            vmem((WIDTH, TOK), BF16),
            vmem((K, WIDTH), BF16),
            vmem((K + 16, VOC), BF16),
            vmem((NY, K, TILE), F32),
            vmem((PEERS, OWN, 256), BF16),
            vmem((PEERS, OWN, 256), BF16),
            vmem((OWN, 128), F32),
            vmem((EX, K * K), F32),
            vmem((PEERS, EX, BLK), BF16),
            vmem((2, PEERS, EX, BLK), BF16),
            vmem((PEERS, EX, BLK), BF16),
            vmem((NZ, 2 * ROWS, BLK), BF16),
            vmem((PEERS, ROWS, BLK), BF16),
            vmem((2, BLK, 128), F32),
            vmem((BLK, 128), F32),
            vmem((BLK, 128), F32),
            dma((4 + NY,)),
            dma, dma,
            dma((3,)), dma((3,)),
            dma((2,)), dma((16,)), dma((15,)),
            dma, dma,
            dma((2,)),
        ],
        compiler_params=pltpu.CompilerParams(
            collective_id=0, has_side_effects=True, vmem_limit_bytes=58 * 1024 * 1024
        ),
        cost_estimate=pl.CostEstimate(flops=500_000_000, bytes_accessed=4_000_000, transcendentals=1_100_000),
    )(logits.T, labels.reshape(NY, TILE), activations.T, proj_in.T, proj_out.T)


def solution(mesh):
    in_specs = (P("dp", "fsdp"), P("dp"), P("dp", "fsdp"), P("fsdp", None), P("fsdp", None))
    out_specs = (P(("dp", "fsdp"), None), P("fsdp", "dp"))
    return jax.shard_map(body, mesh=mesh, in_specs=in_specs, out_specs=out_specs, check_vma=False)
```

```python
import jax
import jax.numpy as jnp
from jax import lax
from jax.experimental import pallas as pl
from jax.experimental.pallas import tpu as pltpu
from jax.sharding import PartitionSpec as P

SEQ = 8
NZ, NX, NY = 8, 4, 4
GROUPS = 16
PEERS = 16
TOK = 512
TILE = 128
OWN = 32
VOC = 2000
WIDTH = 320
K = 64
EX = 4
ROWS = 64
BLK = 256
MESH = pl.DeviceIdType.MESH
F32, BF16 = jnp.float32, jnp.bfloat16


def kernel(
    logits_h, labels_h, act_h, pin_h, pout_h,
    feat, gout,
    logits, labels, act, pin, weights, left,
    psend, psum, xin, yin, lr, pieces, row_in, col_in, rows, cols, acc, xrecv,
    load_sem, rs_send, xin_sem, yin_sem, a2a_send, a2a_recv, ag_send, row_sem, col_sem, x_send, x_recv,
):
    d, f = lax.axis_index("dp"), lax.axis_index("fsdp")
    core, c = lax.rem(d, 2), lax.div(d, 2)
    z, yh = lax.div(c, 2), lax.rem(c, 2)
    yl, x = lax.div(f, NX), lax.rem(f, NX)

    def dev(group, peer):
        return (group * 2 + core, peer)

    quarter = [lax.rem(yl + 1 + s, NY) for s in range(NY)]
    chunks = []
    for s in range(NY):
        at = pl.ds(pl.multiple_of(quarter[s] * TILE, TILE), TILE)
        chunks.append(pltpu.make_async_copy(logits_h.at[:, at], logits.at[s], load_sem.at[4 + s]))
    pairs = ((labels_h, labels), (pout_h, weights.at[0:K]), (pin_h, pin), (act_h, act))
    loads = [pltpu.make_async_copy(src, dst, load_sem.at[k]) for k, (src, dst) in enumerate(pairs)]
    for copy in (chunks[0], loads[0], loads[1], chunks[1], loads[2], loads[3], *chunks[2:]):
        copy.start()

    barrier = pltpu.get_barrier_semaphore()

    def tell(group, peer):
        pl.semaphore_signal(barrier, inc=1, device_id=dev(group, peer), device_id_type=MESH)

    def away(k):
        return lax.rem(z + NZ + k, NZ)

    y_far = z * 2 + 1 - yh
    for k in range(1, NX):
        tell(c, yl * NX + lax.rem(x + k, NX))
    for k in range(1, NY):
        tell(c, lax.rem(yl + k, NY) * NX + x)

    @pl.when(c != f)
    def _():
        tell(f, c)

    tell(y_far, f)
    for k in (-2, -1, 1, 2):
        tell(away(k) * 2 + yh, f)
    other = 1 - core
    partner = (c * 2 + other, f)
    pl.semaphore_signal(barrier, inc=1, device_id=partner, device_id_type=MESH)

    lane = lax.broadcasted_iota(jnp.int32, (1, 128), 1)

    weights[K : K + 16, :] = jnp.ones((16, VOC), BF16)

    def local_tile(s):
        q = quarter[s]
        chunks[s].wait()
        top = logits[s, 0:80, :]
        for at in range(80, VOC, 80):
            top = jnp.maximum(top, logits[s, at : at + 80, :])
        top = jnp.max(top.astype(F32), axis=0, keepdims=True)
        if s == 0:
            loads[0].wait()
            loads[1].wait()
        token = labels[pl.ds(q, 1), :] - f * VOC
        both = jnp.zeros((K + 16, 2 * TILE), F32)
        at_label = jnp.zeros((8, TILE), F32)
        for at in range(0, VOC, 256):
            size = min(256, VOC - at)
            value = logits[s, at : at + size, :].astype(F32)
            hot = lax.broadcasted_iota(jnp.int32, (size, TILE), 0) == token - at
            expo = jnp.where(hot, 0.0, jnp.exp(value - top)).astype(BF16)
            ones = jnp.where(hot, 1.0, 0.0).astype(BF16)
            at_label += jnp.sum(jnp.where(hot, value, 0.0).reshape(size // 8, 8, TILE), axis=0)
            both += jnp.dot(
                weights[:, at : at + size], jnp.concatenate([expo, ones], axis=1), preferred_element_type=F32
            )
        at_label = jnp.sum(at_label, axis=0, keepdims=True)
        total = both[K : K + 16, :TILE]
        low = total - total.astype(BF16).astype(F32)
        wide = (16, TILE)
        a = jnp.concatenate(
            [both[:K, :TILE], total, low, jnp.broadcast_to(top, wide), jnp.broadcast_to(at_label, wide)], axis=0
        )
        b = jnp.concatenate([both[:K, TILE:], left[q]], axis=0)
        a, b = a.T, b.T
        for t in range(NX):
            at = slice(t * OWN, (t + 1) * OWN)
            psend[q * NX + t, :, 0:128] = a[at].astype(BF16)
            psend[q * NX + t, :, 128:256] = b[at].astype(BF16)

    def send_x(s, across):
        pltpu.make_async_remote_copy(
            src_ref=psend.at[quarter[s] * NX + across], dst_ref=xin.at[s, x], send_sem=rs_send,
            recv_sem=xin_sem.at[s], device_id=dev(c, yl * NX + across), device_id_type=MESH,
        ).start()

    def merged(parts):
        parts = [(part[:, 0:128].astype(F32), part[:, 128:256].astype(F32)) for part in parts]
        top = parts[0][0]
        for a, _ in parts[1:]:
            top = jnp.maximum(top, a)
        top = top[:, 96:97]
        sum_a, sum_x, sum_b = (jnp.zeros((OWN, 128), F32) for _ in range(3))
        for a, b in parts:
            sum_a += jnp.exp(a[:, 96:97] - top) * a
            sum_x += a
            sum_b += b
        return top, sum_a, sum_x, sum_b, sum_a[:, 64:65] + sum_a[:, 80:81]

    def merge_x(s):
        xin[s, x] = psend[quarter[s] * NX + x]
        wait_bytes(xin.at[s, pl.ds(0, NX - 1)], xin_sem.at[s])
        top, sum_a, sum_x, sum_b, rest = merged([xin[s, k] for k in range(NX)])
        low = rest - rest.astype(BF16).astype(F32)
        a = jnp.where(lane < 80, jnp.where(lane < K, sum_a, rest), jnp.where(lane < 96, low, top))
        a = jnp.where(lane < 112, a, sum_x)
        return jnp.concatenate([a, sum_b], axis=1).astype(BF16)

    def send_y(s):
        psum[s] = merge_x(s)
        pltpu.make_async_remote_copy(
            src_ref=psum.at[s], dst_ref=yin.at[yl], send_sem=rs_send, recv_sem=yin_sem,
            device_id=dev(c, quarter[s] * NX + x), device_id_type=MESH,
        ).start()

    def wait_bytes(ref, sem):
        pltpu.make_async_copy(ref, ref, sem).wait()

    for s in range(NY):
        if s == 0:
            loads[2].wait()
            loads[3].wait()
            both = jnp.dot(pin[...], act[...], preferred_element_type=F32)
            for q in range(NY):
                left[q] = both[:, q * TILE : (q + 1) * TILE]
        local_tile(s)
        if s == 0:
            @pl.when(c != f)
            def _():
                pl.semaphore_wait(barrier, 13)

            @pl.when(c == f)
            def _():
                pl.semaphore_wait(barrier, 12)

        for t in range(1, NX):
            send_x(s, lax.rem(x + t, NX))
    for s in range(NY - 1):
        send_y(s)
    yin[yl] = merge_x(NY - 1)
    wait_bytes(yin.at[pl.ds(0, NY - 1)], yin_sem)
    top, sum_a, sum_x, sum_b, rest = merged([yin[k] for k in range(NY)])
    total = rest + jnp.exp(sum_x[:, 112:113] - top)
    right = (sum_a - rest * sum_b) / total
    lr[...] = jnp.where(lane < K, right, sum_b)

    halves = []
    for s in range(SEQ // 2):
        both = jnp.concatenate(
            [lr[pl.ds(2 * s, EX, stride=SEQ), :], lr[pl.ds(2 * s + 1, EX, stride=SEQ), :]], axis=0
        )
        halves.append((both, jnp.where(lane < K, both, pltpu.roll(both, K, 1))))
    for k in range(K // 2):
        value = jnp.zeros((8, 128), F32)
        for both, wide in halves:
            first, second = both[:, K + 2 * k : K + 2 * k + 1], both[:, K + 2 * k + 1 : K + 2 * k + 2]
            value += jnp.where(lane < K, first, second) * wide
        value = value[0:EX] + value[EX:8]
        feat[:, k * 128 : (k + 1) * 128] = value
        pieces[k // 2, :, (k % 2) * 128 : (k % 2 + 1) * 128] = value.astype(BF16)

    def send_row(group, block, far):
        pltpu.make_async_remote_copy(
            src_ref=pieces.at[block], dst_ref=row_in.at[far, f], send_sem=a2a_send.at[2 * far],
            recv_sem=a2a_recv.at[2 * far], device_id=dev(group, block), device_id_type=MESH,
        ).start()

    for k in range(1, PEERS):
        send_row(c, lax.rem(f + k, PEERS), 0)
    for k in range(PEERS):
        send_row(y_far, lax.rem(f + k, PEERS), 1)

    def send_col(block):
        pltpu.make_async_remote_copy(
            src_ref=pieces.at[block], dst_ref=col_in.at[f], send_sem=a2a_send.at[1], recv_sem=a2a_recv.at[1],
            device_id=dev(block, c), device_id_type=MESH,
        ).start()

    for k in range(1, PEERS):
        send_col(lax.rem(c + k, PEERS))

    @pl.when(c != f)
    def _():
        send_col(c)

    @pl.when(c == f)
    def _():
        col_in[f] = pieces[c]

    row_in[0, f] = pieces[f]
    wait_bytes(psend.at[pl.ds(0, PEERS - 1)], rs_send)

    def packed(ref):
        lines = [ref[k].astype(F32) for k in range(PEERS)]
        return jnp.concatenate(lines, axis=0).astype(BF16)

    sides = [pl.ds(pl.multiple_of(half * ROWS, ROWS), ROWS) for half in (yh, 1 - yh)]

    def copy_row(origin, far, target, up, hops):
        ref = rows.at[away(origin), sides[far]]
        return pltpu.make_async_remote_copy(
            src_ref=ref, dst_ref=ref, send_sem=ag_send.at[0], recv_sem=row_sem.at[(far * 2 + up) * 4 + hops - 1],
            device_id=dev(away(target) * 2 + yh, f), device_id_type=MESH,
        )

    def row_start(far):
        rows[z, sides[far], :] = packed(row_in.at[far])
        copy_row(0, far, 2, 1, 2).start()
        copy_row(0, far, -2, 0, 2).start()

    def row_pass(far):
        for up, sign in ((1, 1), (0, -1)):
            copy_row(-2 * sign, far, 1, up, 2).wait_recv()
            if up != far:
                copy_row(-2 * sign, far, 2 * sign, up, 4).start()
            copy_row(-2 * sign, far, sign, up, 3).start()

    def copy_col(chunk, target, slot):
        return pltpu.make_async_remote_copy(
            src_ref=cols.at[chunk], dst_ref=cols.at[chunk], send_sem=ag_send.at[1], recv_sem=col_sem.at[slot],
            device_id=dev(c, target), device_id_type=MESH,
        )

    x_up, x_down = lax.rem(x + 1, NX), lax.rem(x + NX - 1, NX)
    x_two = lax.rem(x + 2, NX)

    def col_chunk(k, across):
        return lax.rem(yl + k, NY) * NX + across

    wait_bytes(row_in.at[0, pl.ds(0, PEERS - 1)], a2a_recv.at[0])
    row_start(0)
    wait_bytes(row_in.at[1], a2a_recv.at[2])
    row_start(1)

    @pl.when(c != f)
    def _():
        wait_bytes(col_in, a2a_recv.at[1])

    @pl.when(c == f)
    def _():
        wait_bytes(col_in.at[pl.ds(0, PEERS - 1)], a2a_recv.at[1])

    cols[f] = packed(col_in)
    for k in range(1, NY):
        copy_col(f, lax.rem(yl + k, NY) * NX + x, NY - 1 - k).start()

    def col_send(k):
        copy_col(col_chunk(k, x), yl * NX + x_up, 3 + 3 * k).start()
        copy_col(col_chunk(k, x), yl * NX + x_down, 4 + 3 * k).start()

    def col_pass(k):
        copy_col(col_chunk(k, x_down), yl * NX + x_up, 3 + 3 * k).wait_recv()
        if k % 2 == 0:
            copy_col(col_chunk(k, x_down), yl * NX + x_up, 5 + 3 * k).start()
        copy_col(col_chunk(k, x_up), yl * NX + x_up, 4 + 3 * k).wait_recv()
        if k % 2 == 1:
            copy_col(col_chunk(k, x_up), yl * NX + x_down, 5 + 3 * k).start()

    col_send(0)
    wait_bytes(row_in.at[0, pl.ds(0, PEERS - 1)], a2a_send.at[0])
    wait_bytes(row_in.at[1], a2a_send.at[2])

    @pl.when(c != f)
    def _():
        wait_bytes(pieces, a2a_send.at[1])

    @pl.when(c == f)
    def _():
        wait_bytes(pieces.at[pl.ds(0, PEERS - 1)], a2a_send.at[1])

    for far in (0, 1):
        copy_row(0, far, 1, 1, 1).start()
        copy_row(0, far, -1, 0, 1).start()
    row_pass(0)
    for k in (1, 3, 2):
        copy_col(col_chunk(k, x), f, k - 1).wait_recv()
        col_send(k)
    col_pass(0)
    row_pass(1)
    for k in (1, 3, 2):
        col_pass(k)
    for hops in (1, 3):
        for far in (0, 1):
            for up, sign in ((1, 1), (0, -1)):
                copy_row(-hops * sign, far, 1, up, hops).wait_recv()
    copy_row(-4, 0, 1, 1, 4).wait_recv()
    copy_row(-4, 1, 1, 0, 4).wait_recv()

    def product(at):
        b = cols[pl.ds(at * 2, 2)].reshape(2 * ROWS, BLK)
        return lax.dot_general(rows[at], b, (((0,), (0,)), ((), ())), preferred_element_type=F32)

    total = jnp.zeros((BLK, BLK), F32)
    for k in (0, 1, 3, 2):
        total += product(lax.rem(yl + k, NY) * 2 + lax.div(x, 2))
    for k in (0, 1, 3, 2):
        copy_col(col_chunk(k, x_two), f, 5 + 3 * k).wait_recv()
        total += product(lax.rem(yl + k, NY) * 2 + 1 - lax.div(x, 2))
    acc[0] = total[:, 0:128]
    acc[1] = total[:, 128:256]

    swap = pltpu.make_async_remote_copy(
        src_ref=acc.at[other], dst_ref=xrecv, send_sem=x_send, recv_sem=x_recv,
        device_id=partner, device_id_type=MESH,
    )
    swap.start()
    wait_bytes(rows.at[pl.ds(0, NZ - 1)], ag_send.at[0])
    wait_bytes(cols.at[pl.ds(0, PEERS - 1)], ag_send.at[1])
    swap.wait_recv()
    gout[...] = acc[core] + xrecv[...]
    swap.wait_send()


def body(logits, labels, activations, proj_in, proj_out):
    dma, vmem = pltpu.SemaphoreType.DMA, pltpu.VMEM
    return pl.pallas_call(
        kernel,
        out_shape=(
            jax.ShapeDtypeStruct((EX, K * K), F32),
            jax.ShapeDtypeStruct((BLK, BLK // 2), F32),
        ),
        in_specs=[pl.BlockSpec(memory_space=pltpu.HBM)] * 5,
        out_specs=(pl.BlockSpec(memory_space=pltpu.VMEM),) * 2,
        scratch_shapes=[
            vmem((NY, VOC, TILE), BF16),
            vmem((NY, TILE), jnp.int32),
            vmem((WIDTH, TOK), BF16),
            vmem((K, WIDTH), BF16),
            vmem((K + 16, VOC), BF16),
            vmem((NY, K, TILE), F32),
            vmem((PEERS, OWN, 256), BF16),
            vmem((NY - 1, OWN, 256), BF16),
            vmem((NY, NX, OWN, 256), BF16),
            vmem((NY, OWN, 256), BF16),
            vmem((OWN, 128), F32),
            vmem((PEERS, EX, BLK), BF16),
            vmem((2, PEERS, EX, BLK), BF16),
            vmem((PEERS, EX, BLK), BF16),
            vmem((NZ, 2 * ROWS, BLK), BF16),
            vmem((PEERS, ROWS, BLK), BF16),
            vmem((2, BLK, 128), F32),
            vmem((BLK, 128), F32),
            dma((4 + NY,)),
            dma, dma((NY,)), dma,
            dma((3,)), dma((3,)),
            dma((2,)), dma((16,)), dma((15,)),
            dma, dma,
        ],
        compiler_params=pltpu.CompilerParams(
            collective_id=0, has_side_effects=True, vmem_limit_bytes=40 * 1024 * 1024
        ),
        cost_estimate=pl.CostEstimate(flops=500_000_000, bytes_accessed=4_000_000, transcendentals=1_100_000),
    )(*(
        pltpu.with_memory_space_constraint(a, pltpu.HBM)
        for a in (logits.T, labels.reshape(NY, TILE), activations.T, proj_in.T, proj_out.T)
    ))


def solution(mesh):
    in_specs = (P("dp", "fsdp"), P("dp"), P("dp", "fsdp"), P("fsdp", None), P("fsdp", None))
    out_specs = (P(("dp", "fsdp"), None), P("fsdp", "dp"))
    return jax.shard_map(body, mesh=mesh, in_specs=in_specs, out_specs=out_specs, check_vma=False)
```

```python
import jax
import jax.numpy as jnp
from jax import lax
from jax.experimental import pallas as pl
from jax.experimental.pallas import tpu as pltpu
from jax.sharding import PartitionSpec as P

SEQ = 8
NZ, NX, NY = 8, 4, 4
GROUPS = 16
PEERS = 16
TOK = 512
TILE = 128
OWN = 32
VOC = 2000
WIDTH = 320
K = 64
EX = 4
ROWS = 64
BLK = 256
MESH = pl.DeviceIdType.MESH
F32, BF16 = jnp.float32, jnp.bfloat16


def kernel(
    logits_h, labels_h, act_h, pin_h, pout_h,
    feat, gout,
    logits, labels, act, pin, weights, left,
    psend, psum, xin, yin, lr, pieces, row_in, col_in, rows, cols, acc, xrecv,
    load_sem, rs_send, xin_sem, yin_sem, a2a_send, a2a_recv, ag_send, row_sem, col_sem, x_send, x_recv,
):
    d, f = lax.axis_index("dp"), lax.axis_index("fsdp")
    core, c = lax.rem(d, 2), lax.div(d, 2)
    z, yh = lax.div(c, 2), lax.rem(c, 2)
    yl, x = lax.div(f, NX), lax.rem(f, NX)

    def dev(group, peer):
        return (group * 2 + core, peer)

    quarter = [lax.rem(yl + 1 + s, NY) for s in range(NY)]
    chunks = []
    for s in range(NY):
        at = pl.ds(pl.multiple_of(quarter[s] * TILE, TILE), TILE)
        chunks.append(pltpu.make_async_copy(logits_h.at[:, at], logits.at[s], load_sem.at[4 + s]))
    pairs = ((labels_h, labels), (pout_h, weights.at[0:K]), (pin_h, pin), (act_h, act))
    loads = [pltpu.make_async_copy(src, dst, load_sem.at[k]) for k, (src, dst) in enumerate(pairs)]
    for copy in (chunks[0], loads[0], loads[1], chunks[1], loads[2], loads[3], *chunks[2:]):
        copy.start()

    barrier = pltpu.get_barrier_semaphore()

    def tell(group, peer):
        pl.semaphore_signal(barrier, inc=1, device_id=dev(group, peer), device_id_type=MESH)

    def away(k):
        return lax.rem(z + NZ + k, NZ)

    y_far = z * 2 + 1 - yh
    for k in range(1, NX):
        tell(c, yl * NX + lax.rem(x + k, NX))
    for k in range(1, NY):
        tell(c, lax.rem(yl + k, NY) * NX + x)

    @pl.when(c != f)
    def _():
        tell(f, c)

    tell(y_far, f)
    for k in (-2, -1, 1, 2):
        tell(away(k) * 2 + yh, f)
    other = 1 - core
    partner = (c * 2 + other, f)
    pl.semaphore_signal(barrier, inc=1, device_id=partner, device_id_type=MESH)

    lane = lax.broadcasted_iota(jnp.int32, (1, 128), 1)

    weights[K : K + 16, :] = jnp.ones((16, VOC), BF16)

    def local_tile(s):
        q = quarter[s]
        chunks[s].wait()
        top = logits[s, 0:80, :]
        for at in range(80, VOC, 80):
            top = jnp.maximum(top, logits[s, at : at + 80, :])
        top = jnp.max(top.astype(F32), axis=0, keepdims=True)
        if s == 0:
            loads[0].wait()
            loads[1].wait()
        token = labels[pl.ds(q, 1), :] - f * VOC
        both = jnp.zeros((K + 16, 2 * TILE), F32)
        at_label = jnp.zeros((8, TILE), F32)
        for at in range(0, VOC, 256):
            size = min(256, VOC - at)
            value = logits[s, at : at + size, :].astype(F32)
            hot = lax.broadcasted_iota(jnp.int32, (size, TILE), 0) == token - at
            expo = jnp.where(hot, 0.0, jnp.exp(value - top)).astype(BF16)
            ones = jnp.where(hot, 1.0, 0.0).astype(BF16)
            at_label += jnp.sum(jnp.where(hot, value, 0.0).reshape(size // 8, 8, TILE), axis=0)
            both += jnp.dot(
                weights[:, at : at + size], jnp.concatenate([expo, ones], axis=1), preferred_element_type=F32
            )
        at_label = jnp.sum(at_label, axis=0, keepdims=True)
        total = both[K : K + 16, :TILE]
        low = total - total.astype(BF16).astype(F32)
        wide = (16, TILE)
        a = jnp.concatenate(
            [both[:K, :TILE], total, low, jnp.broadcast_to(top, wide), jnp.broadcast_to(at_label, wide)], axis=0
        )
        b = jnp.concatenate([both[:K, TILE:], left[q]], axis=0)
        a, b = a.T, b.T
        for t in range(NX):
            at = slice(t * OWN, (t + 1) * OWN)
            psend[q * NX + t, :, 0:128] = a[at].astype(BF16)
            psend[q * NX + t, :, 128:256] = b[at].astype(BF16)

    def send_x(s, across):
        pltpu.make_async_remote_copy(
            src_ref=psend.at[quarter[s] * NX + across], dst_ref=xin.at[s, x], send_sem=rs_send,
            recv_sem=xin_sem.at[s], device_id=dev(c, yl * NX + across), device_id_type=MESH,
        ).start()

    def merged(parts):
        parts = [(part[:, 0:128].astype(F32), part[:, 128:256].astype(F32)) for part in parts]
        top = parts[0][0]
        for a, _ in parts[1:]:
            top = jnp.maximum(top, a)
        top = top[:, 96:97]
        sum_a, sum_x, sum_b = (jnp.zeros((OWN, 128), F32) for _ in range(3))
        for a, b in parts:
            sum_a += jnp.exp(a[:, 96:97] - top) * a
            sum_x += a
            sum_b += b
        return top, sum_a, sum_x, sum_b, sum_a[:, 64:65] + sum_a[:, 80:81]

    def merge_x(s):
        xin[s, x] = psend[quarter[s] * NX + x]
        wait_bytes(xin.at[s, pl.ds(0, NX - 1)], xin_sem.at[s])
        top, sum_a, sum_x, sum_b, rest = merged([xin[s, k] for k in range(NX)])
        low = rest - rest.astype(BF16).astype(F32)
        a = jnp.where(lane < 80, jnp.where(lane < K, sum_a, rest), jnp.where(lane < 96, low, top))
        a = jnp.where(lane < 112, a, sum_x)
        return jnp.concatenate([a, sum_b], axis=1).astype(BF16)

    def send_y(s):
        psum[s] = merge_x(s)
        pltpu.make_async_remote_copy(
            src_ref=psum.at[s], dst_ref=yin.at[yl], send_sem=rs_send, recv_sem=yin_sem,
            device_id=dev(c, quarter[s] * NX + x), device_id_type=MESH,
        ).start()

    def wait_bytes(ref, sem):
        pltpu.make_async_copy(ref, ref, sem).wait()

    for s in range(NY):
        if s == 0:
            loads[2].wait()
            loads[3].wait()
            both = jnp.dot(pin[...], act[...], preferred_element_type=F32)
            for q in range(NY):
                left[q] = both[:, q * TILE : (q + 1) * TILE]
        local_tile(s)
        if s == 0:
            @pl.when(c != f)
            def _():
                pl.semaphore_wait(barrier, 13)

            @pl.when(c == f)
            def _():
                pl.semaphore_wait(barrier, 12)

        for t in range(1, NX):
            send_x(s, lax.rem(x + t, NX))
    for s in range(NY - 1):
        send_y(s)
    yin[yl] = merge_x(NY - 1)
    wait_bytes(yin.at[pl.ds(0, NY - 1)], yin_sem)
    top, sum_a, sum_x, sum_b, rest = merged([yin[k] for k in range(NY)])
    total = rest + jnp.exp(sum_x[:, 112:113] - top)
    right = (sum_a - rest * sum_b) / total
    lr[...] = jnp.where(lane < K, right, sum_b)

    halves = []
    for s in range(SEQ // 2):
        both = jnp.concatenate(
            [lr[pl.ds(2 * s, EX, stride=SEQ), :], lr[pl.ds(2 * s + 1, EX, stride=SEQ), :]], axis=0
        )
        halves.append((both, jnp.where(lane < K, both, pltpu.roll(both, K, 1))))
    for k in range(K // 2):
        value = jnp.zeros((8, 128), F32)
        for both, wide in halves:
            first, second = both[:, K + 2 * k : K + 2 * k + 1], both[:, K + 2 * k + 1 : K + 2 * k + 2]
            value += jnp.where(lane < K, first, second) * wide
        feat[:, k * 128 : (k + 1) * 128] = value
        value = value[0:EX] + value[EX:8]
        pieces[k // 2, :, (k % 2) * 128 : (k % 2 + 1) * 128] = value.astype(BF16)

    def send_row(group, block, far):
        pltpu.make_async_remote_copy(
            src_ref=pieces.at[block], dst_ref=row_in.at[far, f], send_sem=a2a_send.at[2 * far],
            recv_sem=a2a_recv.at[2 * far], device_id=dev(group, block), device_id_type=MESH,
        ).start()


    def send_col(block):
        pltpu.make_async_remote_copy(
            src_ref=pieces.at[block], dst_ref=col_in.at[f], send_sem=a2a_send.at[1], recv_sem=a2a_recv.at[1],
            device_id=dev(block, c), device_id_type=MESH,
        ).start()

    for k in range(1, PEERS):
        send_col(lax.rem(c + k, PEERS))

    @pl.when(c != f)
    def _():
        send_col(c)

    @pl.when(c == f)
    def _():
        col_in[f] = pieces[c]

    for k in range(1, PEERS):
        send_row(c, lax.rem(f + k, PEERS), 0)
    for k in range(PEERS):
        send_row(y_far, lax.rem(f + k, PEERS), 1)
    row_in[0, f] = pieces[f]
    wait_bytes(psend.at[pl.ds(0, PEERS - 1)], rs_send)

    def packed(ref):
        lines = [ref[k].astype(F32) for k in range(PEERS)]
        return jnp.concatenate(lines, axis=0).astype(BF16)

    sides = [pl.ds(pl.multiple_of(half * ROWS, ROWS), ROWS) for half in (yh, 1 - yh)]

    def copy_row(origin, far, target, up, hops):
        ref = rows.at[away(origin), sides[far]]
        return pltpu.make_async_remote_copy(
            src_ref=ref, dst_ref=ref, send_sem=ag_send.at[0], recv_sem=row_sem.at[(far * 2 + up) * 4 + hops - 1],
            device_id=dev(away(target) * 2 + yh, f), device_id_type=MESH,
        )

    def row_start(far):
        rows[z, sides[far], :] = packed(row_in.at[far])
        copy_row(0, far, 2, 1, 2).start()
        copy_row(0, far, -2, 0, 2).start()

    def row_pass(far):
        for up, sign in ((1, 1), (0, -1)):
            copy_row(-2 * sign, far, 1, up, 2).wait_recv()
            if up != far:
                copy_row(-2 * sign, far, 2 * sign, up, 4).start()
            copy_row(-2 * sign, far, sign, up, 3).start()

    def copy_col(chunk, target, slot):
        return pltpu.make_async_remote_copy(
            src_ref=cols.at[chunk], dst_ref=cols.at[chunk], send_sem=ag_send.at[1], recv_sem=col_sem.at[slot],
            device_id=dev(c, target), device_id_type=MESH,
        )

    x_up, x_down = lax.rem(x + 1, NX), lax.rem(x + NX - 1, NX)
    x_two = lax.rem(x + 2, NX)

    def col_chunk(k, across):
        return lax.rem(yl + k, NY) * NX + across

    wait_bytes(row_in.at[0, pl.ds(0, PEERS - 1)], a2a_recv.at[0])
    row_start(0)
    wait_bytes(row_in.at[1], a2a_recv.at[2])
    row_start(1)

    @pl.when(c != f)
    def _():
        wait_bytes(col_in, a2a_recv.at[1])

    @pl.when(c == f)
    def _():
        wait_bytes(col_in.at[pl.ds(0, PEERS - 1)], a2a_recv.at[1])

    cols[f] = packed(col_in)
    for k in range(1, NY):
        copy_col(f, lax.rem(yl + k, NY) * NX + x, NY - 1 - k).start()

    def col_send(k):
        copy_col(col_chunk(k, x), yl * NX + x_up, 3 + 3 * k).start()
        copy_col(col_chunk(k, x), yl * NX + x_down, 4 + 3 * k).start()

    def col_pass(k):
        copy_col(col_chunk(k, x_down), yl * NX + x_up, 3 + 3 * k).wait_recv()
        if k % 2 == 0:
            copy_col(col_chunk(k, x_down), yl * NX + x_up, 5 + 3 * k).start()
        copy_col(col_chunk(k, x_up), yl * NX + x_up, 4 + 3 * k).wait_recv()
        if k % 2 == 1:
            copy_col(col_chunk(k, x_up), yl * NX + x_down, 5 + 3 * k).start()

    col_send(0)
    wait_bytes(row_in.at[0, pl.ds(0, PEERS - 1)], a2a_send.at[0])
    wait_bytes(row_in.at[1], a2a_send.at[2])

    @pl.when(c != f)
    def _():
        wait_bytes(pieces, a2a_send.at[1])

    @pl.when(c == f)
    def _():
        wait_bytes(pieces.at[pl.ds(0, PEERS - 1)], a2a_send.at[1])

    for far in (0, 1):
        copy_row(0, far, 1, 1, 1).start()
        copy_row(0, far, -1, 0, 1).start()
    row_pass(0)
    for k in (1, 3, 2):
        copy_col(col_chunk(k, x), f, k - 1).wait_recv()
        col_send(k)
    col_pass(0)
    row_pass(1)
    for k in (1, 3, 2):
        col_pass(k)
    for hops in (1, 3):
        for far in (0, 1):
            for up, sign in ((1, 1), (0, -1)):
                copy_row(-hops * sign, far, 1, up, hops).wait_recv()
    copy_row(-4, 0, 1, 1, 4).wait_recv()
    copy_row(-4, 1, 1, 0, 4).wait_recv()

    def product(at):
        b = cols[pl.ds(at * 2, 2)].reshape(2 * ROWS, BLK)
        return lax.dot_general(rows[at], b, (((0,), (0,)), ((), ())), preferred_element_type=F32)

    total = jnp.zeros((BLK, BLK), F32)
    for k in (0, 1, 3, 2):
        total += product(lax.rem(yl + k, NY) * 2 + lax.div(x, 2))
    for k in (0, 1, 3, 2):
        copy_col(col_chunk(k, x_two), f, 5 + 3 * k).wait_recv()
        total += product(lax.rem(yl + k, NY) * 2 + 1 - lax.div(x, 2))
    acc[0] = total[:, 0:128]
    acc[1] = total[:, 128:256]

    swap = pltpu.make_async_remote_copy(
        src_ref=acc.at[other], dst_ref=xrecv, send_sem=x_send, recv_sem=x_recv,
        device_id=partner, device_id_type=MESH,
    )
    swap.start()
    gout[0] = acc[core]
    wait_bytes(rows.at[pl.ds(0, NZ - 1)], ag_send.at[0])
    wait_bytes(cols.at[pl.ds(0, PEERS - 1)], ag_send.at[1])
    swap.wait_recv()
    gout[1] = xrecv[...]
    swap.wait_send()


def body(logits, labels, activations, proj_in, proj_out):
    dma, vmem = pltpu.SemaphoreType.DMA, pltpu.VMEM
    feat, gram = pl.pallas_call(
        kernel,
        out_shape=(
            jax.ShapeDtypeStruct((2 * EX, K * K), F32),
            jax.ShapeDtypeStruct((2, BLK, BLK // 2), F32),
        ),
        in_specs=[pl.BlockSpec(memory_space=pltpu.HBM)] * 5,
        out_specs=(pl.BlockSpec(memory_space=pltpu.VMEM),) * 2,
        scratch_shapes=[
            vmem((NY, VOC, TILE), BF16),
            vmem((NY, TILE), jnp.int32),
            vmem((WIDTH, TOK), BF16),
            vmem((K, WIDTH), BF16),
            vmem((K + 16, VOC), BF16),
            vmem((NY, K, TILE), F32),
            vmem((PEERS, OWN, 256), BF16),
            vmem((NY - 1, OWN, 256), BF16),
            vmem((NY, NX, OWN, 256), BF16),
            vmem((NY, OWN, 256), BF16),
            vmem((OWN, 128), F32),
            vmem((PEERS, EX, BLK), BF16),
            vmem((2, PEERS, EX, BLK), BF16),
            vmem((PEERS, EX, BLK), BF16),
            vmem((NZ, 2 * ROWS, BLK), BF16),
            vmem((PEERS, ROWS, BLK), BF16),
            vmem((2, BLK, 128), F32),
            vmem((BLK, 128), F32),
            dma((4 + NY,)),
            dma, dma((NY,)), dma,
            dma((3,)), dma((3,)),
            dma((2,)), dma((16,)), dma((15,)),
            dma, dma,
        ],
        compiler_params=pltpu.CompilerParams(
            collective_id=0, has_side_effects=True, vmem_limit_bytes=40 * 1024 * 1024
        ),
        cost_estimate=pl.CostEstimate(flops=500_000_000, bytes_accessed=4_000_000, transcendentals=1_100_000),
    )(*(
        pltpu.with_memory_space_constraint(a, pltpu.HBM)
        for a in (logits.T, labels.reshape(NY, TILE), activations.T, proj_in.T, proj_out.T)
    ))
    return feat[:EX] + feat[EX:], gram[0] + gram[1]


def solution(mesh):
    in_specs = (P("dp", "fsdp"), P("dp"), P("dp", "fsdp"), P("fsdp", None), P("fsdp", None))
    out_specs = (P(("dp", "fsdp"), None), P("fsdp", "dp"))
    return jax.shard_map(body, mesh=mesh, in_specs=in_specs, out_specs=out_specs, check_vma=False)
```
